512 devices in a mesh: sec: 2 (over x_hi), vocab: 32 (over z, x_lo), rows: 8 (over y, core).
Axes of the slice: x: 4 (x_hi: 2, x_lo: 2; x = x_hi * 2 + x_lo), y: 4, z: 16, core: 2. Of those that a mesh axis runs over, the one named last changes fastest.
Arguments:
- logits: bfloat16 [2, 2048, 65536], P('sec', 'rows', 'vocab'), may hold values from -400 to 400
- hidden: bfloat16 [2048, 2048], P('rows', 'sec'), may hold values from -6 to 6
- head_weight: bfloat16 [2048, 65536], P(('sec', 'rows'), 'vocab'), may hold values from -0.125 to 0.125
Outputs:
- hidden_grad: bfloat16 [2, 1024, 2048], P('sec', 'rows', 'vocab')
- weight_grad: bfloat16 [2048, 65536], P(('sec', 'rows'), 'vocab')
The draws below stay inside these ranges and needn't reach their ends.
All inputs are finite; a program needn't handle non-finite values.
Results may differ from the reference program's by a relative error of at most 0.0059.
Values may be sent and summed in bfloat16 or wider, within the bound.
No kernel may reach another device: no remote copies, remote signals or barrier semaphores. Data moves between devices by JAX's collectives and lax.ppermute only.
A program may use at most 64 MiB of HBM per device.

```python
import math
import jax
import jax.numpy as jnp
from jax import lax

D = 2048
R_DEV = 256
V = 65536
ROWS = 2048
N_ROWS = 8


def draw_logits(key, part):
    key = jax.random.fold_in(key, 7)
    subkeys = jax.random.split(key, 3)
    grid_shape = (ROWS, V)
    column = jnp.arange(V, dtype=jnp.float32) / V
    shared_part = jax.random.normal(subkeys[0], grid_shape, jnp.float32)
    own_part = jax.random.normal(subkeys[1], grid_shape, jnp.float32)
    row_scale = jnp.exp(jax.random.uniform(subkeys[2], (ROWS, 1), jnp.float32, math.log(1.5), math.log(15.0)))
    column_rise = 1.1 * column
    target_logits = row_scale * shared_part + column_rise
    draft_logits = row_scale * (0.8 * shared_part + 0.6 * own_part) + column_rise
    stacked = jnp.stack([target_logits, draft_logits])
    return jnp.clip(stacked, -400.0, 400.0).astype(jnp.bfloat16)


def steps_of(own_key, extent, cuts, least, top_value):
    def one(position, parts):
        heights = jax.random.uniform(jax.random.fold_in(jax.random.fold_in(own_key, 6), position), (parts,), jnp.float32, least / len(cuts), top_value / len(cuts))
        return jnp.repeat(jnp.exp(heights), extent[position] // parts).reshape((-1,) + (1,) * (len(extent) - position - 1))

    factor_of = one(*cuts[0])
    for cut in cuts[1:]:
        factor_of = factor_of * one(*cut)
    return factor_of


def normal_values(rng, shape, width, limit, shards=(), kind=jnp.bfloat16):
    gain = steps_of(rng, shape, shards, -0.22, 0.18) if shards else 1.0
    result = jax.random.normal(rng, shape, jnp.float32) * width * gain
    return jnp.minimum(jnp.maximum(result, -limit), limit).astype(kind)


def setup_inputs(seed: int = 0) -> dict:
    splits = jax.random.split(jax.random.key(seed), 4)
    logits = draw_logits(jax.random.fold_in(splits[3], 71), 0)
    hidden = normal_values(splits[1], (ROWS, D), 1.0, 6.0, ((0, 8), (1, 2)))
    head_weight = normal_values(splits[2], (D, V), D ** -0.5, 0.125, ((0, 16), (1, 32)))
    return dict(logits=logits, hidden=hidden, head_weight=head_weight)


loss_scale = 64.0


def normalized(values):
    highest = jnp.max(values, axis=1, keepdims=True)
    weights = jnp.exp(values - highest)
    return weights / jnp.sum(weights, axis=1, keepdims=True)


def reference(logits, hidden, head_weight):
    half_rows = R_DEV // 2
    head_rows = head_weight.T

    def group_step(running, group_index):
        offset = group_index * R_DEV
        target_tile = lax.dynamic_slice_in_dim(logits[0], offset, R_DEV, 0).astype(jnp.float32)
        draft_tile = lax.dynamic_slice_in_dim(logits[1], offset, R_DEV, 0).astype(jnp.float32)
        target_probs = lax.optimization_barrier(normalized(target_tile).astype(jnp.bfloat16))
        draft_probs = lax.optimization_barrier(normalized(draft_tile).astype(jnp.bfloat16))
        grad_tile = (loss_scale * (draft_probs.astype(jnp.float32) - target_probs.astype(jnp.float32))).astype(jnp.bfloat16)
        hidden_rows = lax.dynamic_slice_in_dim(hidden, offset, R_DEV, 0)
        row_grad = jnp.dot(grad_tile, head_rows, preferred_element_type=jnp.float32).astype(jnp.bfloat16)
        running = running + jnp.dot(hidden_rows.T, grad_tile, preferred_element_type=jnp.float32)
        return running, row_grad

    start_grad = jnp.zeros((D, V), jnp.float32)
    weight_total, row_grads = lax.scan(group_step, start_grad, jnp.arange(N_ROWS, dtype=jnp.int32))
    hidden_grad = row_grads.reshape(N_ROWS, 2, half_rows, D).transpose(1, 0, 2, 3).reshape(2, N_ROWS * half_rows, D)
    return hidden_grad, weight_total.astype(jnp.bfloat16)
```

```python
import jax
import jax.numpy as jnp
from jax import lax
from jax.sharding import PartitionSpec as P

loss_scale = 64.0
swap_sec = [(0, 1), (1, 0)]
swap_core = [(i, i ^ 1) for i in range(8)]
same_core = [[0, 2, 4, 6], [1, 3, 5, 7]]


def body(logits, hidden, head_weight):
    f32, bf16 = jnp.float32, jnp.bfloat16
    section = lax.axis_index("sec")
    core = lax.axis_index("rows") % 2
    own = logits[0]
    rows, width = own.shape
    half_rows = rows // 2
    n_vocab = lax.axis_size("vocab")
    groups = lax.axis_size("rows")
    head_rows = head_weight.shape[0]
    piece = head_rows // 4

    blocks = head_weight.reshape(2, 2, piece, width)
    kept = lax.dynamic_index_in_dim(blocks, section, 1, False).reshape(2 * piece, width)
    outgoing = lax.dynamic_index_in_dim(blocks, 1 - section, 1, False).reshape(2 * piece, width)
    received = lax.ppermute(outgoing, "sec", swap_sec)
    peer = lax.ppermute(own, "sec", swap_sec)
    head_kept = lax.all_gather(kept, "rows", tiled=True)
    head_received = lax.all_gather(received, "rows", tiled=True)

    columns = hidden.reshape(rows, groups // 2, 2, head_rows)
    own_columns = lax.dynamic_index_in_dim(columns, core, 2, False).reshape(rows, -1)
    other_columns = lax.dynamic_index_in_dim(columns, 1 - core, 2, False).reshape(rows, -1)
    core_columns = lax.ppermute(other_columns, "rows", swap_core)

    values = own.astype(f32)
    highest = jnp.max(values, axis=1)
    totals = jnp.sum(jnp.exp(values - highest[:, None]), axis=1)
    part = jnp.stack([highest, totals])
    copies = jnp.broadcast_to(part[None], (2 * n_vocab, 2, rows))
    parts = lax.all_to_all(copies, ("sec", "vocab"), 0, 0, tiled=True)
    parts = parts.reshape(2, n_vocab, 2, rows)
    top = jnp.max(parts[:, :, 0], axis=1)
    total = jnp.sum(parts[:, :, 1] * jnp.exp(parts[:, :, 0] - top[:, None]), axis=1)

    def probability(tile, which):
        m = lax.dynamic_index_in_dim(top, which, 0, False)
        t = lax.dynamic_index_in_dim(total, which, 0, False)
        weights = jnp.exp(tile.astype(f32) - m[:, None]) / t[:, None]
        return weights.astype(bf16)

    own_probs, peer_probs = lax.optimization_barrier(
        (probability(own, section), probability(peer, 1 - section))
    )
    direction = (1 - 2 * section).astype(f32)
    difference = peer_probs.astype(f32) - own_probs.astype(f32)
    grad = (loss_scale * (direction * difference)).astype(bf16)

    def terms(head):
        out = lax.dot_general(head, grad, (((1,), (1,)), ((), ())), preferred_element_type=f32)
        return out.astype(bf16).reshape(groups, 2, piece, 2, half_rows)

    first, second = terms(head_kept), terms(head_received)
    lower = jnp.where(section == 0, first, second)
    upper = jnp.where(section == 0, second, first)
    outgoing_terms = jnp.concatenate([lower, upper]).transpose(3, 0, 1, 2, 4)
    outgoing_terms = outgoing_terms.reshape(2 * n_vocab, piece, half_rows)
    incoming_terms = lax.all_to_all(outgoing_terms, ("sec", "vocab"), 0, 0, tiled=True)
    summed = jnp.sum(incoming_terms.reshape(2, n_vocab, piece, half_rows).astype(f32), axis=1)
    hidden_grad = summed.reshape(2 * piece, half_rows).T.astype(bf16)[None]

    core_grad = lax.ppermute(grad, "rows", swap_core)
    dims = (((0,), (0,)), ((), ()))
    weight_part = lax.dot_general(own_columns, grad, dims, preferred_element_type=f32)
    weight_part = weight_part + lax.dot_general(core_columns, core_grad, dims, preferred_element_type=f32)
    weight_part = weight_part.astype(bf16).reshape(groups // 2, head_rows, width)
    weight_parts = lax.all_to_all(weight_part, "rows", 0, 0, axis_index_groups=same_core, tiled=True)
    weight_grad = jnp.sum(weight_parts.astype(f32), axis=0).astype(bf16)
    return hidden_grad, weight_grad


def solution(mesh):
    in_specs = (P("sec", "rows", "vocab"), P("rows", "sec"), P(("sec", "rows"), "vocab"))
    out_specs = (P("sec", "rows", "vocab"), P(("sec", "rows"), "vocab"))
    return jax.shard_map(body, mesh=mesh, in_specs=in_specs, out_specs=out_specs, check_vma=False)
```

```python
import jax
import jax.numpy as jnp
from jax import lax
from jax.experimental import pallas as pl
from jax.experimental.pallas import tpu as pltpu
from jax.sharding import PartitionSpec as P

loss_scale = 64.0
f32, bf16 = jnp.float32, jnp.bfloat16
swap_sec = [(0, 1), (1, 0)]
swap_core = [(i, i ^ 1) for i in range(8)]
near_groups = [
    [256 * sec + 8 * (8 * far + near) + 2 * y + core for sec in range(2) for core in range(2) for near in range(8)]
    for far in range(4)
    for y in range(4)
]
far_groups = [[8 * far + near for far in range(4)] for near in range(8)]


def shifted(value, distance):
    pairs = [(i, (i + 2 * distance) % 8) for i in range(8)]
    return lax.ppermute(value, "rows", pairs)


def spread(value, step):
    pairs = [(2 * y + o, (y + 2 * o + step) % 4 * 2 + y // 2) for y in range(4) for o in range(2)]
    return lax.ppermute(value, "rows", pairs)


def call(kernel, out_shape, micros, name, smem=0, grid=1, in_blocks=None, out_blocks=None, scratch=(), limit=24):
    def spec(array, dimension):
        block = list(array.shape)
        if dimension is not None:
            block[dimension] //= grid
        index = lambda i: tuple(i if d == dimension else 0 for d in range(len(block)))
        return pl.BlockSpec(tuple(block), index)

    def run(*args):
        cuts = in_blocks or [None] * (len(args) - smem)
        outs = jax.tree.leaves(out_shape)
        out_specs = [spec(o, d) for o, d in zip(outs, out_blocks or [None] * len(outs))]
        return pl.pallas_call(
            kernel,
            out_shape=out_shape,
            grid=(grid,),
            in_specs=[pl.BlockSpec(memory_space=pltpu.SMEM)] * smem
            + [spec(x, d) for x, d in zip(args[smem:], cuts)],
            out_specs=out_specs if len(outs) > 1 else out_specs[0],
            scratch_shapes=scratch,
            compiler_params=pltpu.CompilerParams(vmem_limit_bytes=limit * 1024 * 1024),
            cost_estimate=pl.CostEstimate(flops=int(micros * 1.0e9), bytes_accessed=int(micros * 3.0e6), transcendentals=0),
            name=name,
        )(*args)

    return run


def row_of(column):
    return jnp.broadcast_to(column, (column.shape[0], 128)).T[0:1]


def stats_kernel(values_ref, copies_ref):
    rows, width = values_ref.shape
    highest = values_ref[:, 0:128]
    for c in range(128, width, 128):
        highest = jnp.maximum(highest, values_ref[:, c : c + 128])
    highest = jnp.max(highest.astype(f32), axis=1, keepdims=True)
    totals = jnp.zeros((rows, 128), f32)
    for c in range(0, width, 128):
        totals = totals + jnp.exp(values_ref[:, c : c + 128].astype(f32) - highest)
    totals = jnp.sum(totals, axis=1, keepdims=True)
    part = jnp.concatenate([row_of(highest), row_of(totals)])
    copies_ref[...] = jnp.broadcast_to(part[None], copies_ref.shape)


def grad_kernel(place_ref, parts_ref, own_hbm, peer_hbm, grad_ref, own_ref, peer_ref, own_sems, peer_sems):
    section = place_ref[0]
    rows, width = grad_ref.shape
    pieces = own_sems.shape[0]
    piece = rows // pieces
    copies = []
    for i in range(pieces):
        here = pl.ds(i * piece, piece)
        pair = (
            pltpu.make_async_copy(own_hbm.at[here], own_ref.at[here], own_sems.at[i]),
            pltpu.make_async_copy(peer_hbm.at[here], peer_ref.at[here], peer_sems.at[i]),
        )
        for copy in pair:
            copy.start()
        copies.append(pair)

    def whole(which):
        highest, totals = parts_ref[which, :, 0], parts_ref[which, :, 1]
        top = jnp.max(highest, axis=0, keepdims=True)
        total = jnp.sum(totals * jnp.exp(highest - top), axis=0, keepdims=True)
        return jnp.broadcast_to(top, (128, rows)).T, jnp.broadcast_to(1.0 / total, (128, rows)).T

    own_tops, own_scales = whole(section)
    peer_tops, peer_scales = whole(1 - section)
    factor = loss_scale * (1 - 2 * section).astype(f32)
    for i in range(pieces):
        for copy in copies[i]:
            copy.wait()
        first = i * piece
        for c in range(0, width, 128):
            cut = (slice(first, first + piece), slice(c, c + 128))
            own = jnp.exp(own_ref[cut].astype(f32) - own_tops[cut[0]]) * own_scales[cut[0]]
            peer = jnp.exp(peer_ref[cut].astype(f32) - peer_tops[cut[0]]) * peer_scales[cut[0]]
            difference = peer.astype(bf16).astype(f32) - own.astype(bf16).astype(f32)
            grad_ref[cut] = (factor * difference).astype(bf16)


def logit_grad(place, parts, own, peer, micros):
    pieces = 4
    hbm, vmem = pl.BlockSpec(memory_space=pltpu.HBM), pl.BlockSpec(memory_space=pltpu.VMEM)
    sems = pltpu.SemaphoreType.DMA((pieces,))
    return pl.pallas_call(
        grad_kernel,
        out_shape=jax.ShapeDtypeStruct(own.shape, bf16),
        in_specs=[pl.BlockSpec(memory_space=pltpu.SMEM), vmem, hbm, hbm],
        out_specs=vmem,
        scratch_shapes=[pltpu.VMEM(own.shape, bf16), pltpu.VMEM(own.shape, bf16), sems, sems],
        compiler_params=pltpu.CompilerParams(vmem_limit_bytes=24 * 1024 * 1024),
        cost_estimate=pl.CostEstimate(flops=int(micros * 1.0e9), bytes_accessed=int(micros * 3.0e6), transcendentals=0),
        name="logit_grad",
    )(place, parts, own, peer)


def weight_kernel(own_columns_ref, core_columns_ref, own_ref, core_ref, *out_refs):
    sides = (((0,), (0,)), ((), ()))
    terms = lax.dot_general(own_columns_ref[...], own_ref[...], sides, preferred_element_type=f32)
    terms = terms + lax.dot_general(core_columns_ref[...], core_ref[...], sides, preferred_element_type=f32)
    for j, ref in enumerate(out_refs):
        ref[...] = terms[j * 128 : j * 128 + 128].astype(ref.dtype)


def sum_kernel(*refs):
    total = refs[0][...].astype(f32)
    for ref in refs[1:-1]:
        total = total + ref[...].astype(f32)
    refs[-1][...] = total.astype(bf16)


def terms_kernel(place_ref, *refs):
    heads, own_ref, core_ref, out_ref = refs[:4], refs[4], refs[5], refs[6]
    chip, core = place_ref[1], place_ref[2]
    head = jnp.concatenate([ref[...] for ref in heads])
    for o, ref in enumerate((own_ref, core_ref)):
        terms = lax.dot_general(head, ref[...], (((1,), (1,)), ((), ())), preferred_element_type=f32)
        terms = terms.astype(bf16)
        for step in range(4):
            source = (chip + (8 - 2 * core) - step) % 4
            slot = source % 2 * 4 + source // 2 * 2
            for x in range(2):
                first = step * 128 + x * 64
                for s in range(2):
                    out_ref[s, (core + o) % 2, slot + x] = terms[first : first + 64, s * 128 : s * 128 + 128]


def total_kernel(parts_ref, out_ref):
    total = parts_ref[:, 0].astype(f32)
    for i in range(1, parts_ref.shape[1]):
        total = total + parts_ref[:, i].astype(f32)
    out_ref[...] = total.astype(bf16)


def body(logits, hidden, head_weight):
    section = lax.axis_index("sec")
    core = lax.axis_index("rows") % 2
    chip = lax.axis_index("rows") // 2
    own = logits[0]
    rows, width = own.shape
    half_rows = rows // 2
    n_vocab = lax.axis_size("vocab")
    chips = lax.axis_size("rows") // 2
    head_rows = head_weight.shape[0]

    peer = lax.ppermute(own, "sec", swap_sec)
    heads = [spread(head_weight, step) for step in range(chips)]

    def ahead(index):
        offsets = [((chip + j) % chips * 2 + index) * head_rows for j in range(chips)]
        return [lax.dynamic_slice_in_dim(hidden, o, head_rows, 1) for o in offsets]

    own_columns = jnp.concatenate(ahead(core), axis=1)
    core_columns = lax.ppermute(jnp.concatenate(ahead(1 - core), axis=1), "rows", swap_core)

    peer, heads[:2] = lax.optimization_barrier((peer, heads[:2]))

    copies = jax.ShapeDtypeStruct((2 * n_vocab, 2, rows), f32)
    copies = call(stats_kernel, copies, 3, "row_stats", 0, 2, [0], [2])(own)
    parts = lax.all_to_all(copies, ("sec", "vocab"), 0, 0, tiled=True)
    parts = parts.reshape(2, n_vocab, 2, rows)
    place = jnp.stack([section, chip, core]).astype(jnp.int32)
    grad = logit_grad(place, parts, own, peer, 40)

    columns = (own_columns, core_columns)
    grad, heads, columns = lax.optimization_barrier((grad, heads, columns))
    core_grad = lax.ppermute(grad, "rows", swap_core)
    near = jax.ShapeDtypeStruct((2, 2, 8, 64, half_rows), bf16)
    near = call(terms_kernel, near, 3, "hidden_terms", 1)(place, *heads, grad, core_grad)
    near = near.reshape(32, 64, half_rows)
    near = lax.all_to_all(near, ("sec", "vocab", "rows"), 0, 0, axis_index_groups=near_groups, tiled=True)
    far = jax.ShapeDtypeStruct((4, 64, half_rows), bf16)
    far = call(total_kernel, far, 2, "near_total")(near.reshape(4, 8, 64, half_rows))
    far = lax.all_to_all(far, "vocab", 0, 0, axis_index_groups=far_groups, tiled=True)
    hidden_grad = jax.ShapeDtypeStruct((1, 64, half_rows), bf16)
    hidden_grad = call(total_kernel, hidden_grad, 1, "far_total")(far[None]).transpose(0, 2, 1)

    block = lambda kind: jax.ShapeDtypeStruct((head_rows, width), kind)
    outs = (block(bf16),) * chips
    ahead_terms = call(weight_kernel, outs, 4, "weight_terms", 0, 4, [None, None, 1, 1], [1] * 4)(
        *columns, grad, core_grad
    )
    moved = [shifted(ahead_terms[j], j) for j in (2, 1, 3)]
    weight_grad = call(sum_kernel, block(bf16), 100, "weight_total", 0, 2, [0] * 4, [0])(ahead_terms[0], *moved)
    return hidden_grad, weight_grad


def solution(mesh):
    in_specs = (P("sec", "rows", "vocab"), P("rows", "sec"), P(("sec", "rows"), "vocab"))
    out_specs = (P("sec", "rows", "vocab"), P(("sec", "rows"), "vocab"))
    return jax.shard_map(body, mesh=mesh, in_specs=in_specs, out_specs=out_specs, check_vma=False)
```

```python
import jax
import jax.numpy as jnp
from jax import lax
from jax.experimental import pallas as pl
from jax.experimental.pallas import tpu as pltpu
from jax.sharding import PartitionSpec as P

loss_scale = 64.0
f32, bf16 = jnp.float32, jnp.bfloat16
swap_sec = [(0, 1), (1, 0)]
swap_core = [(i, i ^ 1) for i in range(8)]
near_groups = [
    [256 * sec + 8 * (8 * far + near) + 2 * y + core for sec in range(2) for core in range(2) for near in range(8)]
    for far in range(4)
    for y in range(4)
]
far_groups = [[8 * far + near for far in range(4)] for near in range(8)]


def shifted(value, distance):
    pairs = [(i, (i + 2 * distance) % 8) for i in range(8)]
    return lax.ppermute(value, "rows", pairs)


def spread(value, step):
    pairs = [(2 * y + o, (y + 2 * o + step) % 4 * 2 + y // 2) for y in range(4) for o in range(2)]
    return lax.ppermute(value, "rows", pairs)


def call(kernel, out_shape, micros, name, smem=0, grid=1, in_blocks=None, out_blocks=None, scratch=(), limit=24):
    def spec(array, dimension):
        if isinstance(dimension, pl.BlockSpec):
            return dimension
        block = list(array.shape)
        if dimension is not None:
            block[dimension] //= grid
        index = lambda i: tuple(i if d == dimension else 0 for d in range(len(block)))
        return pl.BlockSpec(tuple(block), index)

    def run(*args):
        cuts = in_blocks or [None] * (len(args) - smem)
        outs = jax.tree.leaves(out_shape)
        out_specs = [spec(o, d) for o, d in zip(outs, out_blocks or [None] * len(outs))]
        return pl.pallas_call(
            kernel,
            out_shape=out_shape,
            grid=(grid,),
            in_specs=[pl.BlockSpec(memory_space=pltpu.SMEM)] * smem
            + [spec(x, d) if grid > 1 else pl.BlockSpec(memory_space=pltpu.VMEM) for x, d in zip(args[smem:], cuts)],
            out_specs=out_specs if len(outs) > 1 else out_specs[0],
            scratch_shapes=scratch,
            compiler_params=pltpu.CompilerParams(vmem_limit_bytes=limit * 1024 * 1024),
            cost_estimate=pl.CostEstimate(flops=int(micros * 1.0e9), bytes_accessed=int(micros * 3.0e6), transcendentals=0),
            name=name,
        )(*args)

    return run


def row_of(column):
    return jnp.broadcast_to(column, (column.shape[0], 128)).T[0:1]


def stats_kernel(values_hbm, copies_ref, values_ref, sems):
    rows, width = values_ref.shape
    pieces = sems.shape[0]
    piece = rows // pieces
    copies = []
    for i in range(pieces):
        here = pl.ds(i * piece, piece)
        copies.append(pltpu.make_async_copy(values_hbm.at[here], values_ref.at[here], sems.at[i]))
        copies[i].start()
    tops, sums = [], []
    for i in range(pieces):
        copies[i].wait()
        here = slice(i * piece, i * piece + piece)
        highest = values_ref[here, 0:128]
        for c in range(128, width, 128):
            highest = jnp.maximum(highest, values_ref[here, c : c + 128])
        highest = jnp.max(highest.astype(f32), axis=1, keepdims=True)
        totals = jnp.zeros((piece, 128), f32)
        for c in range(0, width, 128):
            totals = totals + jnp.exp(values_ref[here, c : c + 128].astype(f32) - highest)
        tops.append(highest)
        sums.append(jnp.sum(totals, axis=1, keepdims=True))
    part = jnp.concatenate([row_of(jnp.concatenate(tops)), row_of(jnp.concatenate(sums))])
    copies_ref[...] = jnp.broadcast_to(part[None], copies_ref.shape)


def row_stats(values, copies, micros):
    pieces = 4
    return pl.pallas_call(
        stats_kernel,
        out_shape=jax.ShapeDtypeStruct((copies, 2, values.shape[0]), f32),
        in_specs=[pl.BlockSpec(memory_space=pltpu.HBM)],
        out_specs=pl.BlockSpec(memory_space=pltpu.VMEM),
        scratch_shapes=[pltpu.VMEM(values.shape, bf16), pltpu.SemaphoreType.DMA((pieces,))],
        compiler_params=pltpu.CompilerParams(vmem_limit_bytes=60 * 1024 * 1024),
        cost_estimate=pl.CostEstimate(flops=int(micros * 1.0e9), bytes_accessed=int(micros * 3.0e6), transcendentals=0),
        name="row_stats",
    )(values)


def grad_kernel(place_ref, parts_ref, hidden_ref, own_ref, peer_ref, pair_ref, columns_ref):
    section, chip, core = place_ref[0], place_ref[1], place_ref[2]
    rows, width = own_ref.shape
    for j in range(4):
        first = (chip + j) % 4 * 256
        cut = slice(j * 128, j * 128 + 128)
        columns_ref[:, cut] = hidden_ref[:, pl.ds(pl.multiple_of(first + core * 128, 128), 128)]
        other = hidden_ref[:, pl.ds(pl.multiple_of(first + (1 - core) * 128, 128), 128)]
        pair_ref[:, width + j * 128 : width + j * 128 + 128] = other

    def whole(which):
        highest, totals = parts_ref[which, :, 0], parts_ref[which, :, 1]
        top = jnp.max(highest, axis=0, keepdims=True)
        total = jnp.sum(totals * jnp.exp(highest - top), axis=0, keepdims=True)
        return jnp.broadcast_to(top, (128, rows)).T, jnp.broadcast_to(1.0 / total, (128, rows)).T

    own_tops, own_scales = whole(section)
    peer_tops, peer_scales = whole(1 - section)
    factor = loss_scale * (1 - 2 * section).astype(f32)
    piece = 64
    for first in range(0, rows, piece):
        for c in range(0, width, 128):
            cut = (slice(first, first + piece), slice(c, c + 128))
            own = jnp.exp(own_ref[cut].astype(f32) - own_tops[cut[0]]) * own_scales[cut[0]]
            peer = jnp.exp(peer_ref[cut].astype(f32) - peer_tops[cut[0]]) * peer_scales[cut[0]]
            difference = peer.astype(bf16).astype(f32) - own.astype(bf16).astype(f32)
            pair_ref[cut] = (factor * difference).astype(bf16)


def logit_grad(place, parts, hidden, own, peer, micros):
    rows, width = own.shape
    half = hidden.shape[1] // 2
    vmem = pl.BlockSpec(memory_space=pltpu.VMEM)
    return pl.pallas_call(
        grad_kernel,
        out_shape=(jax.ShapeDtypeStruct((rows, width + half), bf16), jax.ShapeDtypeStruct((rows, half), bf16)),
        in_specs=[pl.BlockSpec(memory_space=pltpu.SMEM), vmem, vmem, vmem, vmem],
        out_specs=(vmem, vmem),
        compiler_params=pltpu.CompilerParams(vmem_limit_bytes=24 * 1024 * 1024),
        cost_estimate=pl.CostEstimate(flops=int(micros * 1.0e9), bytes_accessed=int(micros * 3.0e6), transcendentals=0),
        name="logit_grad",
    )(place, parts, hidden, own, peer)


def weight_kernel(own_columns_ref, core_columns_ref, own_ref, core_ref, *out_refs):
    sides = (((0,), (0,)), ((), ()))
    terms = lax.dot_general(own_columns_ref[...], own_ref[...], sides, preferred_element_type=f32)
    terms = terms + lax.dot_general(core_columns_ref[...], core_ref[...], sides, preferred_element_type=f32)
    for j, ref in enumerate(out_refs):
        ref[...] = terms[j * 128 : j * 128 + 128].astype(ref.dtype)


def sum_kernel(*refs):
    total = refs[0][...].astype(f32)
    for ref in refs[1:-1]:
        total = total + ref[...].astype(f32)
    refs[-1][...] = total.astype(bf16)


def terms_of(place_ref, head_refs, grad_ref, store):
    chip, core = place_ref[1], place_ref[2]
    head = jnp.concatenate([ref[...] for ref in head_refs])
    grad = grad_ref[:, : head.shape[1]]
    terms = lax.dot_general(head, grad, (((1,), (1,)), ((), ())), preferred_element_type=f32)
    terms = terms.astype(bf16)
    for step in range(4):
        source = (chip + (8 - 2 * core) - step) % 4
        slot = source % 2 * 4 + source // 2 * 2
        for x in range(2):
            first = step * 128 + x * 64
            for s in range(2):
                store(s, slot + x, terms[first : first + 64, s * 128 : s * 128 + 128])


def own_terms_kernel(place_ref, *refs):
    def store(s, slot, terms):
        refs[5][s, slot] = terms

    terms_of(place_ref, refs[:4], refs[4], store)


def terms_kernel(place_ref, *refs):
    core, own_ref, out_ref = place_ref[2], refs[5], refs[6]

    def store(s, slot, terms):
        out_ref[s, 1 - core, slot] = terms

    for s in range(2):
        out_ref[s, core] = own_ref[s]
    terms_of(place_ref, refs[:4], refs[4], store)


def total_kernel(parts_ref, out_ref):
    total = parts_ref[:, 0].astype(f32)
    for i in range(1, parts_ref.shape[1]):
        total = total + parts_ref[:, i].astype(f32)
    out_ref[...] = total.astype(bf16)


def body(logits, hidden, head_weight):
    section = lax.axis_index("sec")
    core = lax.axis_index("rows") % 2
    chip = lax.axis_index("rows") // 2
    own = logits[0]
    rows, width = own.shape
    half_rows = rows // 2
    n_vocab = lax.axis_size("vocab")
    chips = lax.axis_size("rows") // 2
    head_rows = head_weight.shape[0]

    peer = lax.ppermute(own, "sec", swap_sec)
    heads = [spread(head_weight, step) for step in range(chips)]

    peer, heads[1], heads[3] = lax.optimization_barrier((peer, heads[1], heads[3]))

    copies = row_stats(own, 2 * n_vocab, 3)
    parts = lax.all_to_all(copies, ("sec", "vocab"), 0, 0, tiled=True)
    parts = parts.reshape(2, n_vocab, 2, rows)
    place = jnp.stack([section, chip, core]).astype(jnp.int32)
    pair, own_columns = logit_grad(place, parts, hidden, own, peer, 40)

    core_pair = lax.ppermute(pair, "rows", swap_core)
    own_terms = jax.ShapeDtypeStruct((2, 8, 64, half_rows), bf16)
    own_terms = call(own_terms_kernel, own_terms, 40, "own_terms", 1)(place, *heads, pair)
    near = jax.ShapeDtypeStruct((2, 2, 8, 64, half_rows), bf16)
    near = call(terms_kernel, near, 2, "hidden_terms", 1)(place, *heads, core_pair, own_terms)
    near = near.reshape(32, 64, half_rows)
    near = lax.all_to_all(near, ("sec", "vocab", "rows"), 0, 0, axis_index_groups=near_groups, tiled=True)
    far = jax.ShapeDtypeStruct((4, 64, half_rows), bf16)
    far = call(total_kernel, far, 2, "near_total")(near.reshape(4, 8, 64, half_rows))
    far = lax.all_to_all(far, "vocab", 0, 0, axis_index_groups=far_groups, tiled=True)
    hidden_grad = jax.ShapeDtypeStruct((1, 64, half_rows), bf16)
    hidden_grad = call(total_kernel, hidden_grad, 1, "far_total")(far[None]).transpose(0, 2, 1)

    block = lambda kind: jax.ShapeDtypeStruct((head_rows, width), kind)
    outs = (block(bf16),) * chips
    quarter = width // 4
    columns = pl.BlockSpec((rows, quarter), lambda i: (0, 4))
    tile = pl.BlockSpec((rows, quarter), lambda i: (0, i))
    ahead_terms = call(weight_kernel, outs, 4, "weight_terms", 0, 4, [None, columns, tile, tile], [1] * 4)(
        own_columns, core_pair, pair, core_pair
    )
    moved = [shifted(ahead_terms[j], j) for j in (2, 1, 3)]
    weight_grad = call(sum_kernel, block(bf16), 100, "weight_total", 0, 2, [0] * 4, [0])(ahead_terms[0], *moved)
    return hidden_grad, weight_grad


def solution(mesh):
    in_specs = (P("sec", "rows", "vocab"), P("rows", "sec"), P(("sec", "rows"), "vocab"))
    out_specs = (P("sec", "rows", "vocab"), P(("sec", "rows"), "vocab"))
    return jax.shard_map(body, mesh=mesh, in_specs=in_specs, out_specs=out_specs, check_vma=False)
```

```python
import jax
import jax.numpy as jnp
from jax import lax
from jax.experimental import pallas as pl
from jax.experimental.pallas import tpu as pltpu
from jax.sharding import PartitionSpec as P

loss_scale = 64.0
f32, bf16 = jnp.float32, jnp.bfloat16
swap_sec = [(0, 1), (1, 0)]
swap_core = [(i, i ^ 1) for i in range(8)]
near_groups = [
    [256 * sec + 8 * (8 * far + near) + 2 * y + core for sec in range(2) for core in range(2) for near in range(8)]
    for far in range(4)
    for y in range(4)
]
far_groups = [[8 * far + near for far in range(4)] for near in range(8)]


def shifted(value, distance):
    pairs = [(i, (i + 2 * distance) % 8) for i in range(8)]
    return lax.ppermute(value, "rows", pairs)


def spread(value, step):
    pairs = [(2 * y + o, (y + 2 * o + step) % 4 * 2 + y // 2) for y in range(4) for o in range(2)]
    return lax.ppermute(value, "rows", pairs)


def call(kernel, out_shape, micros, name, smem=0, grid=1, in_blocks=None, out_blocks=None, scratch=(), limit=24, whole=False):
    def spec(array, dimension):
        if isinstance(dimension, pl.BlockSpec):
            return dimension
        block = list(array.shape)
        if dimension is not None:
            block[dimension] //= grid
        index = lambda i: tuple(i if d == dimension else 0 for d in range(len(block)))
        return pl.BlockSpec(tuple(block), index)

    def run(*args):
        cuts = in_blocks or [None] * (len(args) - smem)
        outs = jax.tree.leaves(out_shape)
        out_specs = [spec(o, d) for o, d in zip(outs, out_blocks or [None] * len(outs))]
        if whole:
            out_specs = [pl.BlockSpec(memory_space=pltpu.VMEM)] * len(outs)
        return pl.pallas_call(
            kernel,
            out_shape=out_shape,
            grid=(grid,),
            in_specs=[pl.BlockSpec(memory_space=pltpu.SMEM)] * smem
            + [spec(x, d) if grid > 1 or d else pl.BlockSpec(memory_space=pltpu.VMEM) for x, d in zip(args[smem:], cuts)],
            out_specs=out_specs if len(outs) > 1 else out_specs[0],
            scratch_shapes=scratch,
            compiler_params=pltpu.CompilerParams(vmem_limit_bytes=limit * 1024 * 1024),
            cost_estimate=pl.CostEstimate(flops=int(micros * 1.0e9), bytes_accessed=int(micros * 3.0e6), transcendentals=0),
            name=name,
        )(*args)

    return run


def row_of(column):
    return jnp.broadcast_to(column, (column.shape[0], 128)).T[0:1]


def stats_kernel(values_hbm, copies_ref, values_ref, sems):
    rows, width = values_ref.shape
    pieces = sems.shape[0]
    piece = rows // pieces
    copies = []
    for i in range(pieces):
        here = pl.ds(i * piece, piece)
        copies.append(pltpu.make_async_copy(values_hbm.at[here], values_ref.at[here], sems.at[i]))
        copies[i].start()
    parts = []
    for i in range(pieces):
        copies[i].wait()
        here = slice(i * piece, i * piece + piece)
        highest = values_ref[here, 0:128]
        for c in range(128, width, 128):
            highest = jnp.maximum(highest, values_ref[here, c : c + 128])
        highest = jnp.max(highest.astype(f32), axis=1, keepdims=True)
        totals = jnp.zeros((piece, 128), f32)
        for c in range(0, width, 128):
            totals = totals + jnp.exp(values_ref[here, c : c + 128].astype(f32) - highest)
        totals = jnp.sum(totals, axis=1, keepdims=True)
        parts.append(jnp.concatenate([row_of(highest), row_of(totals)]))
    part = jnp.concatenate(parts, axis=1)
    copies_ref[...] = jnp.broadcast_to(part[None], copies_ref.shape)


def row_stats(values, copies, micros):
    pieces = 2
    return pl.pallas_call(
        stats_kernel,
        out_shape=jax.ShapeDtypeStruct((copies, 2, values.shape[0]), f32),
        in_specs=[pl.BlockSpec(memory_space=pltpu.HBM)],
        out_specs=pl.BlockSpec(memory_space=pltpu.VMEM),
        scratch_shapes=[pltpu.VMEM(values.shape, bf16), pltpu.SemaphoreType.DMA((pieces,))],
        compiler_params=pltpu.CompilerParams(vmem_limit_bytes=60 * 1024 * 1024),
        cost_estimate=pl.CostEstimate(flops=int(micros * 1.0e9), bytes_accessed=int(micros * 3.0e6), transcendentals=0),
        name="row_stats",
    )(values)


def grad_kernel(place_ref, parts_ref, hidden_ref, own_ref, peer_ref, pair_ref, columns_ref):
    section, chip, core = place_ref[0], place_ref[1], place_ref[2]
    rows, width = own_ref.shape
    for j in range(4):
        first = (chip + j) % 4 * 256
        cut = slice(j * 128, j * 128 + 128)
        columns_ref[:, cut] = hidden_ref[:, pl.ds(pl.multiple_of(first + core * 128, 128), 128)]
        other = hidden_ref[:, pl.ds(pl.multiple_of(first + (1 - core) * 128, 128), 128)]
        pair_ref[:, width + j * 128 : width + j * 128 + 128] = other

    def whole(which):
        highest, totals = parts_ref[which, :, 0], parts_ref[which, :, 1]
        top = jnp.max(highest, axis=0, keepdims=True)
        total = jnp.sum(totals * jnp.exp(highest - top), axis=0, keepdims=True)
        return jnp.broadcast_to(top, (128, rows)).T, jnp.broadcast_to(1.0 / total, (128, rows)).T

    own_tops, own_scales = whole(section)
    peer_tops, peer_scales = whole(1 - section)
    factor = loss_scale * (1 - 2 * section).astype(f32)
    piece = 64
    for first in range(0, rows, piece):
        for c in range(0, width, 128):
            cut = (slice(first, first + piece), slice(c, c + 128))
            own = jnp.exp(own_ref[cut].astype(f32) - own_tops[cut[0]]) * own_scales[cut[0]]
            peer = jnp.exp(peer_ref[cut].astype(f32) - peer_tops[cut[0]]) * peer_scales[cut[0]]
            difference = peer.astype(bf16).astype(f32) - own.astype(bf16).astype(f32)
            pair_ref[cut] = (factor * difference).astype(bf16)


def logit_grad(place, parts, hidden, own, peer, micros):
    rows, width = own.shape
    half = hidden.shape[1] // 2
    vmem = pl.BlockSpec(memory_space=pltpu.VMEM)
    return pl.pallas_call(
        grad_kernel,
        out_shape=(jax.ShapeDtypeStruct((rows, width + half), bf16), jax.ShapeDtypeStruct((rows, half), bf16)),
        in_specs=[pl.BlockSpec(memory_space=pltpu.SMEM), vmem, vmem, vmem, vmem],
        out_specs=(vmem, vmem),
        compiler_params=pltpu.CompilerParams(vmem_limit_bytes=24 * 1024 * 1024),
        cost_estimate=pl.CostEstimate(flops=int(micros * 1.0e9), bytes_accessed=int(micros * 3.0e6), transcendentals=0),
        name="logit_grad",
    )(place, parts, hidden, own, peer)


def weight_kernel(own_columns_ref, own_ref, core_ref, *out_refs):
    sides = (((0,), (0,)), ((), ()))
    width = out_refs[0].shape[1]
    for first in range(0, width, 512):
        cut = slice(first, first + 512)
        terms = lax.dot_general(own_columns_ref[...], own_ref[:, cut], sides, preferred_element_type=f32)
        terms = terms + lax.dot_general(core_ref[:, width:], core_ref[:, cut], sides, preferred_element_type=f32)
        for j, ref in enumerate(out_refs):
            ref[:, cut] = terms[j * 128 : j * 128 + 128].astype(ref.dtype)


def sum_kernel(*refs):
    total = refs[0][...].astype(f32)
    for ref in refs[1:-1]:
        total = total + ref[...].astype(f32)
    refs[-1][...] = total.astype(bf16)


def terms_of(place_ref, head, grad_ref, store):
    chip, core = place_ref[1], place_ref[2]
    grad = grad_ref[:, : head.shape[1]]
    terms = lax.dot_general(head, grad, (((1,), (1,)), ((), ())), preferred_element_type=f32)
    terms = terms.astype(bf16)
    for step in range(4):
        source = (chip + (8 - 2 * core) - step) % 4
        slot = source % 2 * 4 + source // 2 * 2
        for x in range(2):
            first = step * 128 + x * 64
            for s in range(2):
                store(s, slot + x, terms[first : first + 64, s * 128 : s * 128 + 128])


def own_terms_kernel(place_ref, *refs):
    grad_ref, out_ref, head_ref = refs[4:]
    for i in range(4):
        head_ref[i * 128 : i * 128 + 128] = refs[i][...]

    def store(s, slot, terms):
        out_ref[s, slot] = terms

    terms_of(place_ref, head_ref[...], grad_ref, store)


def terms_kernel(place_ref, head_ref, grad_ref, own_ref, unread_ref, out_hbm, terms_ref, sems):
    core = place_ref[2]

    def store(s, slot, terms):
        terms_ref[s, slot] = terms

    copies = [pltpu.make_async_copy(own_ref.at[s], out_hbm.at[s, core], sems.at[s]) for s in range(2)]
    for copy in copies:
        copy.start()
    terms_of(place_ref, head_ref[...], grad_ref, store)
    for s in range(2):
        copies.append(pltpu.make_async_copy(terms_ref.at[s], out_hbm.at[s, 1 - core], sems.at[2 + s]))
        copies[-1].start()
    for copy in copies:
        copy.wait()


def hidden_terms(place, head, grad, own_terms, unread, micros):
    vmem, anywhere = pl.BlockSpec(memory_space=pltpu.VMEM), pl.BlockSpec(memory_space=pl.ANY)
    shape = own_terms.shape
    return pl.pallas_call(
        terms_kernel,
        out_shape=jax.ShapeDtypeStruct((shape[0], 2) + shape[1:], bf16),
        in_specs=[pl.BlockSpec(memory_space=pltpu.SMEM), vmem, vmem, vmem, anywhere],
        out_specs=pl.BlockSpec(memory_space=pltpu.HBM),
        scratch_shapes=[pltpu.VMEM(shape, bf16), pltpu.SemaphoreType.DMA((4,))],
        compiler_params=pltpu.CompilerParams(vmem_limit_bytes=24 * 1024 * 1024),
        cost_estimate=pl.CostEstimate(flops=int(micros * 1.0e9), bytes_accessed=int(micros * 3.0e6), transcendentals=0),
        name="hidden_terms",
    )(place, head, grad, own_terms, unread)


def total_kernel(parts_ref, out_ref):
    total = parts_ref[:, 0].astype(f32)
    for i in range(1, parts_ref.shape[1]):
        total = total + parts_ref[:, i].astype(f32)
    out_ref[...] = total.astype(bf16)


def body(logits, hidden, head_weight):
    section = lax.axis_index("sec")
    core = lax.axis_index("rows") % 2
    chip = lax.axis_index("rows") // 2
    own = logits[0]
    rows, width = own.shape
    half_rows = rows // 2
    n_vocab = lax.axis_size("vocab")
    chips = lax.axis_size("rows") // 2
    head_rows = head_weight.shape[0]

    peer = lax.ppermute(own, "sec", swap_sec)
    heads = [spread(head_weight, step) for step in range(chips)]

    peer, heads[1], heads[3] = lax.optimization_barrier((peer, heads[1], heads[3]))

    copies = row_stats(own, 2 * n_vocab, 3)
    parts = lax.all_to_all(copies, ("sec", "vocab"), 0, 0, tiled=True)
    parts = parts.reshape(2, n_vocab, 2, rows)
    place = jnp.stack([section, chip, core]).astype(jnp.int32)
    pair, own_columns = logit_grad(place, parts, hidden, own, peer, 40)

    core_pair = lax.ppermute(pair, "rows", swap_core)
    own_terms = jax.ShapeDtypeStruct((2, 8, 64, half_rows), bf16)
    head = jax.ShapeDtypeStruct((chips * head_rows, width), bf16)
    own_terms, head = call(own_terms_kernel, (own_terms, head), 40, "own_terms", 1, whole=True)(place, *heads, pair)
    block = lambda kind: jax.ShapeDtypeStruct((head_rows, width), kind)
    outs = (block(bf16),) * chips
    ahead_terms = call(weight_kernel, outs, 4, "weight_terms")(own_columns, pair, core_pair)
    near = hidden_terms(place, head, core_pair, own_terms, ahead_terms[0], 2)
    near = near.reshape(32, 64, half_rows)
    near = lax.all_to_all(near, ("sec", "vocab", "rows"), 0, 0, axis_index_groups=near_groups, tiled=True)
    far = jax.ShapeDtypeStruct((4, 64, half_rows), bf16)
    far = call(total_kernel, far, 2, "near_total")(near.reshape(4, 8, 64, half_rows))
    far = lax.all_to_all(far, "vocab", 0, 0, axis_index_groups=far_groups, tiled=True)
    hidden_grad = jax.ShapeDtypeStruct((1, 64, half_rows), bf16)
    hidden_grad = call(total_kernel, hidden_grad, 1, "far_total")(far[None]).transpose(0, 2, 1)

    moved = [shifted(ahead_terms[j], j) for j in (2, 1, 3)]
    weight_grad = call(sum_kernel, block(bf16), 100, "weight_total", 0, 2, [0] * 4, [0])(ahead_terms[0], *moved)
    return hidden_grad, weight_grad


def solution(mesh):
    in_specs = (P("sec", "rows", "vocab"), P("rows", "sec"), P(("sec", "rows"), "vocab"))
    out_specs = (P("sec", "rows", "vocab"), P(("sec", "rows"), "vocab"))
    return jax.shard_map(body, mesh=mesh, in_specs=in_specs, out_specs=out_specs, check_vma=False)
```

```python
import jax
import jax.numpy as jnp
from jax import lax
from jax.experimental import pallas as pl
from jax.experimental.pallas import tpu as pltpu
from jax.sharding import PartitionSpec as P

loss_scale = 64.0
f32, bf16 = jnp.float32, jnp.bfloat16
swap_sec = [(0, 1), (1, 0)]
swap_core = [(i, i ^ 1) for i in range(8)]
near_groups = [
    [256 * sec + 8 * (8 * far + near) + 2 * y + core for sec in range(2) for core in range(2) for near in range(8)]
    for far in range(4)
    for y in range(4)
]
far_groups = [[8 * far + near for far in range(4)] for near in range(8)]


def shifted(value, distance):
    pairs = [(i, (i + 2 * distance) % 8) for i in range(8)]
    return lax.ppermute(value, "rows", pairs)


def spread(value, step):
    pairs = [(2 * y + o, (y + 2 * o + step) % 4 * 2 + y // 2) for y in range(4) for o in range(2)]
    return lax.ppermute(value, "rows", pairs)


def call(kernel, out_shape, micros, name, smem=0, grid=1, in_blocks=None, out_blocks=None, scratch=(), limit=24, whole=False):
    def spec(array, dimension):
        if isinstance(dimension, pl.BlockSpec):
            return dimension
        block = list(array.shape)
        if dimension is not None:
            block[dimension] //= grid
        index = lambda i: tuple(i if d == dimension else 0 for d in range(len(block)))
        return pl.BlockSpec(tuple(block), index)

    def run(*args):
        cuts = in_blocks or [None] * (len(args) - smem)
        outs = jax.tree.leaves(out_shape)
        out_specs = [spec(o, d) for o, d in zip(outs, out_blocks or [None] * len(outs))]
        if whole:
            out_specs = [pl.BlockSpec(memory_space=pltpu.VMEM)] * len(outs)
        return pl.pallas_call(
            kernel,
            out_shape=out_shape,
            grid=(grid,),
            in_specs=[pl.BlockSpec(memory_space=pltpu.SMEM)] * smem
            + [spec(x, d) if grid > 1 or d else pl.BlockSpec(memory_space=pltpu.VMEM) for x, d in zip(args[smem:], cuts)],
            out_specs=out_specs if len(outs) > 1 else out_specs[0],
            scratch_shapes=scratch,
            compiler_params=pltpu.CompilerParams(vmem_limit_bytes=limit * 1024 * 1024),
            cost_estimate=pl.CostEstimate(flops=int(micros * 1.0e9), bytes_accessed=int(micros * 3.0e6), transcendentals=0),
            name=name,
        )(*args)

    return run


def row_of(column):
    return jnp.broadcast_to(column, (column.shape[0], 128)).T[0:1]


def stats_kernel(values_hbm, copies_ref, values_ref, sems):
    rows, width = values_ref.shape
    pieces = sems.shape[0]
    piece = rows // pieces
    copies = []
    for i in range(pieces):
        here = pl.ds(i * piece, piece)
        copies.append(pltpu.make_async_copy(values_hbm.at[here], values_ref.at[here], sems.at[i]))
        copies[i].start()
    tops, sums = [], []
    for i in range(pieces):
        copies[i].wait()
        here = slice(i * piece, i * piece + piece)
        lanes = values_ref[here, 0:128]
        for c in range(128, width, 128):
            lanes = jnp.maximum(lanes, values_ref[here, c : c + 128])
        lanes = lanes.astype(f32)
        totals = jnp.zeros((piece, 128), f32)
        for c in range(0, width, 128):
            totals = totals + jnp.exp(values_ref[here, c : c + 128].astype(f32) - lanes)
        tops.append(lanes)
        sums.append(totals)
    lanes = jnp.concatenate(tops).T
    totals = jnp.concatenate(sums).T
    highest = jnp.max(lanes, axis=0, keepdims=True)
    total = jnp.sum(totals * jnp.exp(lanes - highest), axis=0, keepdims=True)
    part = jnp.concatenate([highest, total])
    copies_ref[...] = jnp.broadcast_to(part[None], copies_ref.shape)


def row_stats(values, copies, micros):
    pieces = 4
    return pl.pallas_call(
        stats_kernel,
        out_shape=jax.ShapeDtypeStruct((copies, 2, values.shape[0]), f32),
        in_specs=[pl.BlockSpec(memory_space=pltpu.HBM)],
        out_specs=pl.BlockSpec(memory_space=pltpu.VMEM),
        scratch_shapes=[pltpu.VMEM(values.shape, bf16), pltpu.SemaphoreType.DMA((pieces,))],
        compiler_params=pltpu.CompilerParams(vmem_limit_bytes=60 * 1024 * 1024),
        cost_estimate=pl.CostEstimate(flops=int(micros * 1.0e9), bytes_accessed=int(micros * 3.0e6), transcendentals=0),
        name="row_stats",
    )(values)


def grad_kernel(place_ref, parts_ref, hidden_ref, own_ref, peer_ref, pair_ref, columns_ref):
    section, chip, core = place_ref[0], place_ref[1], place_ref[2]
    rows, width = own_ref.shape
    for j in range(4):
        first = (chip + j) % 4 * 256
        cut = slice(j * 128, j * 128 + 128)
        columns_ref[:, cut] = hidden_ref[:, pl.ds(pl.multiple_of(first + core * 128, 128), 128)]
        other = hidden_ref[:, pl.ds(pl.multiple_of(first + (1 - core) * 128, 128), 128)]
        pair_ref[:, width + j * 128 : width + j * 128 + 128] = other

    def whole(which):
        highest, totals = parts_ref[which, :, 0], parts_ref[which, :, 1]
        top = jnp.max(highest, axis=0, keepdims=True)
        total = jnp.sum(totals * jnp.exp(highest - top), axis=0, keepdims=True)
        return jnp.broadcast_to(top, (128, rows)).T, jnp.broadcast_to(1.0 / total, (128, rows)).T

    own_tops, own_scales = whole(section)
    peer_tops, peer_scales = whole(1 - section)
    factor = loss_scale * (1 - 2 * section).astype(f32)
    piece = 64
    for first in range(0, rows, piece):
        for c in range(0, width, 128):
            cut = (slice(first, first + piece), slice(c, c + 128))
            own = jnp.exp(own_ref[cut].astype(f32) - own_tops[cut[0]]) * own_scales[cut[0]]
            peer = jnp.exp(peer_ref[cut].astype(f32) - peer_tops[cut[0]]) * peer_scales[cut[0]]
            difference = peer.astype(bf16).astype(f32) - own.astype(bf16).astype(f32)
            pair_ref[cut] = (factor * difference).astype(bf16)


def logit_grad(place, parts, hidden, own, peer, micros):
    rows, width = own.shape
    half = hidden.shape[1] // 2
    vmem = pl.BlockSpec(memory_space=pltpu.VMEM)
    return pl.pallas_call(
        grad_kernel,
        out_shape=(jax.ShapeDtypeStruct((rows, width + half), bf16), jax.ShapeDtypeStruct((rows, half), bf16)),
        in_specs=[pl.BlockSpec(memory_space=pltpu.SMEM), vmem, vmem, vmem, vmem],
        out_specs=(vmem, vmem),
        compiler_params=pltpu.CompilerParams(vmem_limit_bytes=24 * 1024 * 1024),
        cost_estimate=pl.CostEstimate(flops=int(micros * 1.0e9), bytes_accessed=int(micros * 3.0e6), transcendentals=0),
        name="logit_grad",
    )(place, parts, hidden, own, peer)


def weight_kernel(own_columns_ref, own_ref, core_ref, *out_refs):
    sides = (((0,), (0,)), ((), ()))
    width = out_refs[0].shape[1]
    for first in range(0, width, 512):
        cut = slice(first, first + 512)
        terms = lax.dot_general(own_columns_ref[...], own_ref[:, cut], sides, preferred_element_type=f32)
        terms = terms + lax.dot_general(core_ref[:, width:], core_ref[:, cut], sides, preferred_element_type=f32)
        for j, ref in enumerate(out_refs):
            ref[:, cut] = terms[j * 128 : j * 128 + 128].astype(ref.dtype)


def sum_kernel(*refs):
    total = refs[0][...].astype(f32)
    for ref in refs[1:-1]:
        total = total + ref[...].astype(f32)
    refs[-1][...] = total.astype(bf16)


def terms_of(place_ref, head, grad_ref, store):
    chip, core = place_ref[1], place_ref[2]
    grad = grad_ref[:, : head.shape[1]]
    terms = lax.dot_general(head, grad, (((1,), (1,)), ((), ())), preferred_element_type=f32)
    terms = terms.astype(bf16)
    for step in range(4):
        source = (chip + (8 - 2 * core) - step) % 4
        slot = source % 2 * 4 + source // 2 * 2
        for x in range(2):
            first = step * 128 + x * 64
            for s in range(2):
                store(s, slot + x, terms[first : first + 64, s * 128 : s * 128 + 128])


def own_terms_kernel(place_ref, *refs):
    grad_ref, out_ref, head_ref = refs[4:]
    for i in range(4):
        head_ref[i * 128 : i * 128 + 128] = refs[i][...]

    def store(s, slot, terms):
        out_ref[s, slot] = terms

    terms_of(place_ref, head_ref[...], grad_ref, store)


def terms_kernel(place_ref, head_ref, grad_ref, own_ref, out_hbm, terms_ref, sems):
    core = place_ref[2]

    def store(s, slot, terms):
        terms_ref[s, slot] = terms

    copies = [pltpu.make_async_copy(own_ref.at[s], out_hbm.at[s, core], sems.at[s]) for s in range(2)]
    for copy in copies:
        copy.start()
    terms_of(place_ref, head_ref[...], grad_ref, store)
    for s in range(2):
        copies.append(pltpu.make_async_copy(terms_ref.at[s], out_hbm.at[s, 1 - core], sems.at[2 + s]))
        copies[-1].start()
    for copy in copies:
        copy.wait()


def hidden_terms(place, head, grad, own_terms, micros):
    vmem = pl.BlockSpec(memory_space=pltpu.VMEM)
    shape = own_terms.shape
    return pl.pallas_call(
        terms_kernel,
        out_shape=jax.ShapeDtypeStruct((shape[0], 2) + shape[1:], bf16),
        in_specs=[pl.BlockSpec(memory_space=pltpu.SMEM), vmem, vmem, vmem],
        out_specs=pl.BlockSpec(memory_space=pltpu.HBM),
        scratch_shapes=[pltpu.VMEM(shape, bf16), pltpu.SemaphoreType.DMA((4,))],
        compiler_params=pltpu.CompilerParams(vmem_limit_bytes=24 * 1024 * 1024),
        cost_estimate=pl.CostEstimate(flops=int(micros * 1.0e9), bytes_accessed=int(micros * 3.0e6), transcendentals=0),
        name="hidden_terms",
    )(place, head, grad, own_terms)


def total_kernel(parts_ref, out_ref):
    total = parts_ref[:, 0].astype(f32)
    for i in range(1, parts_ref.shape[1]):
        total = total + parts_ref[:, i].astype(f32)
    out_ref[...] = total.astype(bf16)


def body(logits, hidden, head_weight):
    section = lax.axis_index("sec")
    core = lax.axis_index("rows") % 2
    chip = lax.axis_index("rows") // 2
    own = logits[0]
    rows, width = own.shape
    half_rows = rows // 2
    n_vocab = lax.axis_size("vocab")
    chips = lax.axis_size("rows") // 2
    head_rows = head_weight.shape[0]

    peer = lax.ppermute(own, "sec", swap_sec)
    heads = [spread(head_weight, step) for step in range(chips)]

    peer, heads[1], heads[3] = lax.optimization_barrier((peer, heads[1], heads[3]))

    copies = row_stats(own, 2 * n_vocab, 3)
    parts = lax.all_to_all(copies, ("sec", "vocab"), 0, 0, tiled=True)
    parts = parts.reshape(2, n_vocab, 2, rows)
    place = jnp.stack([section, chip, core]).astype(jnp.int32)
    pair, own_columns = logit_grad(place, parts, hidden, own, peer, 40)

    core_pair = lax.ppermute(pair, "rows", swap_core)
    own_terms = jax.ShapeDtypeStruct((2, 8, 64, half_rows), bf16)
    head = jax.ShapeDtypeStruct((chips * head_rows, width), bf16)
    own_terms, head = call(own_terms_kernel, (own_terms, head), 40, "own_terms", 1, whole=True)(place, *heads, pair)
    block = lambda kind: jax.ShapeDtypeStruct((head_rows, width), kind)
    outs = (block(bf16),) * chips
    ahead_terms = call(weight_kernel, outs, 4, "weight_terms")(own_columns, pair, core_pair)
    near = hidden_terms(place, head, core_pair, own_terms, 2)
    near = near.reshape(32, 64, half_rows)
    near = lax.all_to_all(near, ("sec", "vocab", "rows"), 0, 0, axis_index_groups=near_groups, tiled=True)
    far = jax.ShapeDtypeStruct((4, 64, half_rows), bf16)
    far = call(total_kernel, far, 2, "near_total")(near.reshape(4, 8, 64, half_rows))
    far = lax.all_to_all(far, "vocab", 0, 0, axis_index_groups=far_groups, tiled=True)
    hidden_grad = jax.ShapeDtypeStruct((1, 64, half_rows), bf16)
    hidden_grad = call(total_kernel, hidden_grad, 1, "far_total")(far[None]).transpose(0, 2, 1)

    moved = [shifted(ahead_terms[j], j) for j in (2, 1, 3)]
    weight_grad = call(sum_kernel, block(bf16), 100, "weight_total", 0, 2, [0] * 4, [0])(ahead_terms[0], *moved)
    return hidden_grad, weight_grad


def solution(mesh):
    in_specs = (P("sec", "rows", "vocab"), P("rows", "sec"), P(("sec", "rows"), "vocab"))
    out_specs = (P("sec", "rows", "vocab"), P(("sec", "rows"), "vocab"))
    return jax.shard_map(body, mesh=mesh, in_specs=in_specs, out_specs=out_specs, check_vma=False)
```

```python
import functools

import jax
import jax.numpy as jnp
from jax import lax
from jax.experimental import pallas as pl
from jax.experimental.pallas import tpu as pltpu
from jax.sharding import PartitionSpec as P

loss_scale = 64.0
f32, bf16 = jnp.float32, jnp.bfloat16
swap_sec = [(0, 1), (1, 0)]
swap_core = [(i, i ^ 1) for i in range(8)]
near_groups = [
    [256 * sec + 8 * (8 * far + near) + 2 * y + core for sec in range(2) for core in range(2) for near in range(8)]
    for far in range(4)
    for y in range(4)
]
far_groups = [[8 * far + near for far in range(4)] for near in range(8)]


def shifted(value, distance):
    pairs = [(i, (i + 2 * distance) % 8) for i in range(8)]
    return lax.ppermute(value, "rows", pairs)


def spread(value, step):
    pairs = [(2 * y + o, (y + 2 * o + step) % 4 * 2 + y // 2) for y in range(4) for o in range(2)]
    return lax.ppermute(value, "rows", pairs)


def call(kernel, out_shape, micros, name, smem=0, grid=1, in_blocks=None, out_blocks=None, scratch=(), limit=24, whole=False):
    def spec(array, dimension):
        if isinstance(dimension, pl.BlockSpec):
            return dimension
        block = list(array.shape)
        if dimension is not None:
            block[dimension] //= grid
        index = lambda i: tuple(i if d == dimension else 0 for d in range(len(block)))
        return pl.BlockSpec(tuple(block), index)

    def run(*args):
        cuts = in_blocks or [None] * (len(args) - smem)
        outs = jax.tree.leaves(out_shape)
        out_specs = [spec(o, d) for o, d in zip(outs, out_blocks or [None] * len(outs))]
        if whole:
            out_specs = [pl.BlockSpec(memory_space=pltpu.VMEM)] * len(outs)
        return pl.pallas_call(
            kernel,
            out_shape=out_shape,
            grid=(grid,),
            in_specs=[pl.BlockSpec(memory_space=pltpu.SMEM)] * smem
            + [spec(x, d) if grid > 1 or d else pl.BlockSpec(memory_space=pltpu.VMEM) for x, d in zip(args[smem:], cuts)],
            out_specs=out_specs if len(outs) > 1 else out_specs[0],
            scratch_shapes=scratch,
            compiler_params=pltpu.CompilerParams(vmem_limit_bytes=limit * 1024 * 1024),
            cost_estimate=pl.CostEstimate(flops=int(micros * 1.0e9), bytes_accessed=int(micros * 3.0e6), transcendentals=0),
            name=name,
        )(*args)

    return run


def row_of(column):
    return jnp.broadcast_to(column, (column.shape[0], 128)).T[0:1]


def stats_kernel(values_hbm, copies_ref, values_ref, sems):
    rows, width = values_ref.shape
    pieces = sems.shape[0]
    piece = rows // pieces
    copies = []
    for i in range(pieces):
        here = pl.ds(i * piece, piece)
        copies.append(pltpu.make_async_copy(values_hbm.at[here], values_ref.at[here], sems.at[i]))
        copies[i].start()
    tops, sums = [], []
    for i in range(pieces):
        copies[i].wait()
        here = slice(i * piece, i * piece + piece)
        lanes = values_ref[here, 0:128]
        for c in range(128, width, 128):
            lanes = jnp.maximum(lanes, values_ref[here, c : c + 128])
        lanes = lanes.astype(f32)
        totals = jnp.zeros((piece, 128), f32)
        for c in range(0, width, 128):
            totals = totals + jnp.exp(values_ref[here, c : c + 128].astype(f32) - lanes)
        tops.append(lanes)
        sums.append(totals)
    lanes = jnp.concatenate(tops).T
    totals = jnp.concatenate(sums).T
    highest = jnp.max(lanes, axis=0, keepdims=True)
    total = jnp.sum(totals * jnp.exp(lanes - highest), axis=0, keepdims=True)
    part = jnp.concatenate([highest, total])
    copies_ref[...] = jnp.broadcast_to(part[None], copies_ref.shape)


def row_stats(values, copies, micros):
    pieces = 4
    return pl.pallas_call(
        stats_kernel,
        out_shape=jax.ShapeDtypeStruct((copies, 2, values.shape[0]), f32),
        in_specs=[pl.BlockSpec(memory_space=pltpu.HBM)],
        out_specs=pl.BlockSpec(memory_space=pltpu.VMEM),
        scratch_shapes=[pltpu.VMEM(values.shape, bf16), pltpu.SemaphoreType.DMA((pieces,))],
        compiler_params=pltpu.CompilerParams(vmem_limit_bytes=60 * 1024 * 1024),
        cost_estimate=pl.CostEstimate(flops=int(micros * 1.0e9), bytes_accessed=int(micros * 3.0e6), transcendentals=0),
        name="row_stats",
    )(values)


def grad_kernel(place_ref, parts_ref, hidden_ref, own_ref, peer_ref, pair_ref, columns_ref):
    section, chip, core = place_ref[0], place_ref[1], place_ref[2]
    rows, width = own_ref.shape
    for j in range(4):
        first = (chip + j) % 4 * 256
        cut = slice(j * 128, j * 128 + 128)
        columns_ref[:, cut] = hidden_ref[:, pl.ds(pl.multiple_of(first + core * 128, 128), 128)]
        other = hidden_ref[:, pl.ds(pl.multiple_of(first + (1 - core) * 128, 128), 128)]
        pair_ref[:, width + j * 128 : width + j * 128 + 128] = other

    def whole(which):
        highest, totals = parts_ref[which, :, 0], parts_ref[which, :, 1]
        top = jnp.max(highest, axis=0, keepdims=True)
        total = jnp.sum(totals * jnp.exp(highest - top), axis=0, keepdims=True)
        return jnp.broadcast_to(top, (128, rows)).T, jnp.broadcast_to(1.0 / total, (128, rows)).T

    own_tops, own_scales = whole(section)
    peer_tops, peer_scales = whole(1 - section)
    factor = loss_scale * (1 - 2 * section).astype(f32)
    piece = 64
    for first in range(0, rows, piece):
        for c in range(0, width, 128):
            cut = (slice(first, first + piece), slice(c, c + 128))
            own = jnp.exp(own_ref[cut].astype(f32) - own_tops[cut[0]]) * own_scales[cut[0]]
            peer = jnp.exp(peer_ref[cut].astype(f32) - peer_tops[cut[0]]) * peer_scales[cut[0]]
            difference = peer.astype(bf16).astype(f32) - own.astype(bf16).astype(f32)
            pair_ref[cut] = (factor * difference).astype(bf16)


def logit_grad(place, parts, hidden, own, peer, micros):
    rows, width = own.shape
    half = hidden.shape[1] // 2
    vmem = pl.BlockSpec(memory_space=pltpu.VMEM)
    return pl.pallas_call(
        grad_kernel,
        out_shape=(jax.ShapeDtypeStruct((rows, width + half), bf16), jax.ShapeDtypeStruct((rows, half), bf16)),
        in_specs=[pl.BlockSpec(memory_space=pltpu.SMEM), vmem, vmem, vmem, vmem],
        out_specs=(vmem, vmem),
        compiler_params=pltpu.CompilerParams(vmem_limit_bytes=24 * 1024 * 1024),
        cost_estimate=pl.CostEstimate(flops=int(micros * 1.0e9), bytes_accessed=int(micros * 3.0e6), transcendentals=0),
        name="logit_grad",
    )(place, parts, hidden, own, peer)


def weight_kernel(ahead, own_columns_ref, own_ref, core_ref, *out_refs):
    sides = (((0,), (0,)), ((), ()))
    width = out_refs[0].shape[1]
    here = slice(ahead[0] * 128, ahead[-1] * 128 + 128)
    there = slice(width + ahead[0] * 128, width + ahead[-1] * 128 + 128)
    for first in range(0, width, 512):
        cut = slice(first, first + 512)
        terms = lax.dot_general(own_columns_ref[:, here], own_ref[:, cut], sides, preferred_element_type=f32)
        terms = terms + lax.dot_general(core_ref[:, there], core_ref[:, cut], sides, preferred_element_type=f32)
        for i, ref in enumerate(out_refs):
            ref[:, cut] = terms[i * 128 : i * 128 + 128].astype(ref.dtype)


def sum_kernel(*refs):
    total = refs[0][...].astype(f32)
    for ref in refs[1:-1]:
        total = total + ref[...].astype(f32)
    refs[-1][...] = total.astype(bf16)


def terms_of(place_ref, head, grad_ref, store):
    chip, core = place_ref[1], place_ref[2]
    grad = grad_ref[:, : head.shape[1]]
    terms = lax.dot_general(head, grad, (((1,), (1,)), ((), ())), preferred_element_type=f32)
    terms = terms.astype(bf16)
    for step in range(4):
        source = (chip + (8 - 2 * core) - step) % 4
        slot = source % 2 * 4 + source // 2 * 2
        for x in range(2):
            first = step * 128 + x * 64
            for s in range(2):
                store(s, slot + x, terms[first : first + 64, s * 128 : s * 128 + 128])


def own_terms_kernel(place_ref, *refs):
    grad_ref, out_ref, head_ref = refs[4:]
    for i in range(4):
        head_ref[i * 128 : i * 128 + 128] = refs[i][...]

    def store(s, slot, terms):
        out_ref[s, slot] = terms

    terms_of(place_ref, head_ref[...], grad_ref, store)


def terms_kernel(place_ref, head_ref, grad_ref, own_ref, out_hbm, terms_ref, sems):
    core = place_ref[2]

    def store(s, slot, terms):
        terms_ref[s, slot] = terms

    copies = [pltpu.make_async_copy(own_ref.at[s], out_hbm.at[s, core], sems.at[s]) for s in range(2)]
    for copy in copies:
        copy.start()
    terms_of(place_ref, head_ref[...], grad_ref, store)
    for s in range(2):
        copies.append(pltpu.make_async_copy(terms_ref.at[s], out_hbm.at[s, 1 - core], sems.at[2 + s]))
        copies[-1].start()
    for copy in copies:
        copy.wait()


def hidden_terms(place, head, grad, own_terms, micros):
    vmem = pl.BlockSpec(memory_space=pltpu.VMEM)
    shape = own_terms.shape
    return pl.pallas_call(
        terms_kernel,
        out_shape=jax.ShapeDtypeStruct((shape[0], 2) + shape[1:], bf16),
        in_specs=[pl.BlockSpec(memory_space=pltpu.SMEM), vmem, vmem, vmem],
        out_specs=pl.BlockSpec(memory_space=pltpu.HBM),
        scratch_shapes=[pltpu.VMEM(shape, bf16), pltpu.SemaphoreType.DMA((4,))],
        compiler_params=pltpu.CompilerParams(vmem_limit_bytes=24 * 1024 * 1024),
        cost_estimate=pl.CostEstimate(flops=int(micros * 1.0e9), bytes_accessed=int(micros * 3.0e6), transcendentals=0),
        name="hidden_terms",
    )(place, head, grad, own_terms)


def total_kernel(parts_ref, out_ref):
    total = parts_ref[:, 0].astype(f32)
    for i in range(1, parts_ref.shape[1]):
        total = total + parts_ref[:, i].astype(f32)
    out_ref[...] = total.astype(bf16)


def body(logits, hidden, head_weight):
    section = lax.axis_index("sec")
    core = lax.axis_index("rows") % 2
    chip = lax.axis_index("rows") // 2
    own = logits[0]
    rows, width = own.shape
    half_rows = rows // 2
    n_vocab = lax.axis_size("vocab")
    chips = lax.axis_size("rows") // 2
    head_rows = head_weight.shape[0]

    peer = lax.ppermute(own, "sec", swap_sec)
    heads = [spread(head_weight, step) for step in range(chips)]

    peer, heads[1], heads[3] = lax.optimization_barrier((peer, heads[1], heads[3]))

    copies = row_stats(own, 2 * n_vocab, 3)
    parts = lax.all_to_all(copies, ("sec", "vocab"), 0, 0, tiled=True)
    parts = parts.reshape(2, n_vocab, 2, rows)
    place = jnp.stack([section, chip, core]).astype(jnp.int32)
    pair, own_columns = logit_grad(place, parts, hidden, own, peer, 40)

    core_pair = lax.ppermute(pair, "rows", swap_core)
    own_terms = jax.ShapeDtypeStruct((2, 8, 64, half_rows), bf16)
    head = jax.ShapeDtypeStruct((chips * head_rows, width), bf16)
    own_terms, head = call(own_terms_kernel, (own_terms, head), 40, "own_terms", 1, whole=True)(place, *heads, pair)
    block = lambda kind: jax.ShapeDtypeStruct((head_rows, width), kind)
    sent, stays = functools.partial(weight_kernel, (1, 2, 3)), functools.partial(weight_kernel, (0,))
    ahead_terms = call(sent, (block(bf16),) * 3, 3, "weight_terms")(own_columns, pair, core_pair)
    near = hidden_terms(place, head, core_pair, own_terms, 2)
    near = near.reshape(32, 64, half_rows)
    near = lax.all_to_all(near, ("sec", "vocab", "rows"), 0, 0, axis_index_groups=near_groups, tiled=True)
    far = jax.ShapeDtypeStruct((4, 64, half_rows), bf16)
    far = call(total_kernel, far, 2, "near_total")(near.reshape(4, 8, 64, half_rows))
    far = lax.all_to_all(far, "vocab", 0, 0, axis_index_groups=far_groups, tiled=True)
    hidden_grad = jax.ShapeDtypeStruct((1, 64, half_rows), bf16)
    hidden_grad = call(total_kernel, hidden_grad, 1, "far_total")(far[None]).transpose(0, 2, 1)

    moved = [shifted(ahead_terms[j - 1], j) for j in (2, 1, 3)]
    own_block = call(stays, block(bf16), 1, "own_weight_terms")(own_columns, pair, core_pair)
    weight_grad = call(sum_kernel, block(bf16), 100, "weight_total", 0, 2, [0] * 4, [0])(own_block, *moved)
    return hidden_grad, weight_grad


def solution(mesh):
    in_specs = (P("sec", "rows", "vocab"), P("rows", "sec"), P(("sec", "rows"), "vocab"))
    out_specs = (P("sec", "rows", "vocab"), P(("sec", "rows"), "vocab"))
    return jax.shard_map(body, mesh=mesh, in_specs=in_specs, out_specs=out_specs, check_vma=False)
```
